512 devices in a mesh: seq: 32 (over z, x), chan: 16 (over y, core).
Axes of the slice: x: 4, y: 8, z: 8, core: 2. Of those that a mesh axis runs over, the one named last changes fastest.
Arguments:
- streams: bfloat16 [3, 16384, 4096], P(None, 'seq', 'chan'), may hold values from -6 to 6
- short_weight: float32 [3, 3, 4096], P(None, None, 'chan'), may hold values from -3 to 3
- short_bias: float32 [3, 4096], P(None, 'chan'), may hold values from -3 to 3
- spectrum: bfloat16 [2, 2, 16384, 4096], P(None, None, ('chan', 'seq')), may hold values from -6 to 6
- skip_gain: float32 [4096], P('chan'), may hold values from -4 to 4
Outputs:
- mixed: bfloat16 [16384, 4096], P('seq', 'chan')
The draws below stay inside these ranges and needn't reach their ends.
All inputs are finite; a program needn't handle non-finite values.
Results may differ from the reference program's by a relative error of at most 0.01.
Values may be sent and summed in bfloat16 or wider, within the bound.
No kernel may reach another device: no remote copies, remote signals or barrier semaphores. Data moves between devices by JAX's collectives and lax.ppermute only.
A program may use at most 64 MiB of HBM per device.

```python
import math
import jax
import jax.numpy as jnp
from jax import lax

D = 4096
TOKENS = 16384


def shard_levels(key, extent, cuts, least, high):
    factor_of = 1.0
    for position, blocks in cuts:
        draws = jax.random.uniform(jax.random.fold_in(jax.random.fold_in(key, 6), position), (blocks,), jnp.float32, least / len(cuts), high / len(cuts))
        factor_of = factor_of * jnp.repeat(jnp.exp(draws), extent[position] // blocks).reshape((-1,) + (1,) * (len(extent) - 1 - position))
    return factor_of


def bell_draw(stream_key, dims, deviation, most, cuts=(), kind=jnp.bfloat16):
    array = deviation * jax.random.normal(stream_key, dims, jnp.float32)
    if cuts:
        array = array * shard_levels(stream_key, dims, cuts, -0.22, 0.18)
    return jnp.clip(array, -most, most).astype(kind)


def setup_inputs(seed: int = 0) -> dict:
    key_list = jax.random.split(jax.random.key(seed), 6)
    return {
        "streams": bell_draw(key_list[0], (3, TOKENS, D), 1.0, 6.0, ((1, 32), (2, 16))),
        "short_weight": bell_draw(key_list[1], (3, 3, D), 0.5, 3.0, ((2, 16),), jnp.float32),
        "short_bias": bell_draw(key_list[2], (3, D), 0.5, 3.0, ((1, 16),), jnp.float32),
        "spectrum": bell_draw(key_list[3], (2, 2, TOKENS, D), 1.0, 6.0, ((2, 512),)),
        "skip_gain": bell_draw(key_list[4], (D,), 1.0, 4.0, ((0, 16),), jnp.float32),
    }


def reference(streams, short_weight, short_bias, spectrum, skip_gain):
    values = streams.astype(jnp.float32)
    length = values.shape[1]
    width = values.shape[2]
    padded = jnp.pad(values, ((0, 0), (2, 0), (0, 0)))
    short_out = (short_weight[0][:, None, :] * padded[:, 2:, :]
                 + short_weight[1][:, None, :] * padded[:, 1:-1, :]
                 + short_weight[2][:, None, :] * padded[:, :-2, :]
                 + short_bias[:, None, :])
    gated_input = (short_out[1] * short_out[2]).astype(jnp.bfloat16)
    signal = gated_input.astype(jnp.float32)
    real_part = jnp.transpose(spectrum[:, 0], (1, 0, 2)).reshape(2 * length, width).astype(jnp.float32)
    imag_part = jnp.transpose(spectrum[:, 1], (1, 0, 2)).reshape(2 * length, width).astype(jnp.float32)
    group_width = math.gcd(width, 256)
    group_count = width // group_width

    def into_groups(array_in):
        return array_in.reshape(array_in.shape[0], group_count, group_width).transpose(1, 0, 2)

    def convolve(members):
        piece_signal, piece_real, piece_imag = members
        transformed = jnp.fft.fft(piece_signal, n=2 * length, axis=0)
        weighted = transformed * lax.complex(piece_real, piece_imag)
        return jnp.real(jnp.fft.ifft(weighted, axis=0))[:length]

    convolved = lax.map(convolve, (into_groups(signal), into_groups(real_part), into_groups(imag_part)))
    convolved = convolved.transpose(1, 0, 2).reshape(length, width)
    return ((convolved + signal * skip_gain[None, :]) * short_out[0]).astype(jnp.bfloat16)
```

```python
import functools

import jax
import jax.numpy as jnp
import numpy as np
from jax import lax
from jax.experimental import pallas as pl
from jax.experimental.pallas import tpu as pltpu
from jax.sharding import PartitionSpec as P

F32 = jnp.float32
BF16 = jnp.bfloat16
VMEM_LIMIT = 56 * 1024 * 1024


def dot_t(lhs, rhs):
    return lax.dot_general(lhs, rhs, (((1,), (1,)), ((), ())), preferred_element_type=F32)


def dot(lhs, rhs):
    return jnp.dot(lhs, rhs, preferred_element_type=F32)


class Plan:
    def __init__(self, seq, chans, tokens, channels):
        self.seq = seq
        self.own = channels // (seq * chans)
        self.span = tokens // seq
        self.total = 2 * tokens
        self.lows = 2 * seq
        self.rows = self.own * self.lows

    def low_order(self):
        q = np.arange(self.lows)
        half = self.lows // 2
        return 2 * (q % half) + q // half

    def first_table(self):
        low = self.low_order()
        s = np.arange(self.seq)
        angle = 2.0 * np.pi * ((low[:, None] * s[None, :]) % self.lows) / self.lows
        eye = np.eye(self.own)
        parts = np.stack([np.cos(angle), np.sin(angle)])
        full = np.einsum("pqs,cd->pcqsd", parts, eye)
        return full.reshape(2 * self.rows, self.seq * self.own)

    def last_table(self):
        low = self.low_order()
        s = np.arange(self.seq)
        angle = 2.0 * np.pi * ((low[:, None] * s[None, :]) % self.lows) / self.lows
        eye = np.eye(self.own)
        parts = np.stack([np.cos(angle), -np.sin(angle)])
        full = np.einsum("pqs,cd->sdpcq", parts, eye)
        return full.reshape(self.seq * self.own, 2 * self.rows)

    def big_table(self):
        d = np.arange(self.span)
        angle = 2.0 * np.pi * ((d[:, None] * d[None, :]) % self.span) / self.span
        c, s = np.cos(angle), np.sin(angle)
        return np.block([[c, -s], [s, c]])

    def twiddle(self):
        low = self.low_order()
        a = np.arange(self.span)
        angle = 2.0 * np.pi * ((low[:, None] * a[None, :]) % self.total) / self.total
        return np.stack([np.cos(angle), np.sin(angle)])


def spectrum_kernel(spec_ref, eye_ref, out_ref):
    eye = eye_ref[...]
    rows = [spec_ref[r, i] for i in range(2) for r in range(2)]
    block = jnp.concatenate(rows, axis=0)
    width = eye.shape[0]
    for j in range(block.shape[1] // width):
        piece = block[:, j * width : (j + 1) * width]
        out_ref[j * width : (j + 1) * width, :] = dot_t(eye, piece).astype(BF16)


def transpose_spectrum(spectrum, eye, per_step):
    rows = 4 * spectrum.shape[2]
    chans = spectrum.shape[3]
    return pl.pallas_call(
        spectrum_kernel,
        grid=(chans // per_step,),
        in_specs=[
            pl.BlockSpec((2, 2, spectrum.shape[2], per_step), lambda g: (0, 0, 0, g)),
            pl.BlockSpec(eye.shape, lambda g: (0, 0)),
        ],
        out_specs=pl.BlockSpec((per_step, rows), lambda g: (g, 0)),
        out_shape=jax.ShapeDtypeStruct((chans, rows), BF16),
        cost_estimate=pl.CostEstimate(
            flops=2 * rows * chans * eye.shape[0], bytes_accessed=4 * rows * chans, transcendentals=0
        ),
        name="transpose_spectrum",
    )(spectrum, eye)


def conv_kernel(streams_ref, halo_ref, weight_ref, bias_ref, eye_ref, u_ref, ut_ref, gate_ref):
    length = streams_ref.shape[1]
    row = lax.broadcasted_iota(jnp.int32, (length, streams_ref.shape[2]), 0)

    def short(k):
        now = streams_ref[k].astype(F32)
        halo = halo_ref[k].astype(F32)
        one = jnp.where(row == 0, halo[1:2, :], pltpu.roll(now, 1, 0))
        two = pltpu.roll(now, 2, 0)
        two = jnp.where(row == 0, halo[0:1, :], jnp.where(row == 1, halo[1:2, :], two))
        return (
            weight_ref[0, k : k + 1, :] * now
            + weight_ref[1, k : k + 1, :] * one
            + weight_ref[2, k : k + 1, :] * two
            + bias_ref[k : k + 1, :]
        )

    u = (short(1) * short(2)).astype(BF16)
    u_ref[...] = u
    ut_ref[...] = dot_t(eye_ref[...], u).astype(BF16)
    gate_ref[...] = short(0)


def short_conv(streams, halo, weight, bias, eye):
    _, length, chans = streams.shape
    return pl.pallas_call(
        conv_kernel,
        out_shape=(
            jax.ShapeDtypeStruct((length, chans), BF16),
            jax.ShapeDtypeStruct((chans, length), BF16),
            jax.ShapeDtypeStruct((length, chans), F32),
        ),
        cost_estimate=pl.CostEstimate(
            flops=2 * length * chans * chans, bytes_accessed=14 * length * chans, transcendentals=0
        ),
        compiler_params=pltpu.CompilerParams(vmem_limit_bytes=VMEM_LIMIT),
        name="short_conv",
    )(streams, halo, weight, bias, eye)


def filter_kernel(recv_ref, out_ref, wide_ref):
    depth, own, lanes = recv_ref.shape
    half = lanes // 2
    wide_ref[...] = recv_ref[...].astype(F32)
    first = lax.broadcasted_iota(jnp.int32, (depth, lanes), 1) < half
    for pair in range(own // 2):
        even = wide_ref[:, 2 * pair, :]
        odd = wide_ref[:, 2 * pair + 1, :]
        span = slice(pair * lanes, (pair + 1) * lanes)
        out_ref[:depth, span] = jnp.where(first, even, pltpu.roll(odd, half, 1))
        out_ref[depth:, span] = jnp.where(first, pltpu.roll(even, half, 1), odd)


def arrange_filter(recv):
    depth, own, lanes = recv.shape
    return pl.pallas_call(
        filter_kernel,
        out_shape=jax.ShapeDtypeStruct((2 * depth, own * lanes // 2), F32),
        scratch_shapes=[pltpu.VMEM((depth, own, lanes), F32)],
        cost_estimate=pl.CostEstimate(
            flops=4 * depth * own * lanes, bytes_accessed=6 * depth * own * lanes, transcendentals=0
        ),
        compiler_params=pltpu.CompilerParams(vmem_limit_bytes=VMEM_LIMIT),
        name="arrange_filter",
    )(recv)


def transform_kernel(plan, u_ref, filt_ref, first_ref, big_ref, tw_ref, twt_ref, last_ref, y_ref, g_ref, yf_ref, b_ref):
    span, lows, own, rows = plan.span, plan.lows, plan.own, plan.rows
    u = u_ref[...]
    for c in range(own):
        re = dot(first_ref[c * lows : (c + 1) * lows, :], u)
        im = dot(first_ref[rows + c * lows : rows + (c + 1) * lows, :], u)
        g_ref[c * lows : (c + 1) * lows, :span] = (re * tw_ref[0] - im * tw_ref[1]).astype(BF16)
        g_ref[c * lows : (c + 1) * lows, span:] = (re * tw_ref[1] + im * tw_ref[0]).astype(BF16)
    lanes = 2 * lows
    block = 2 * lanes
    for j in range(rows // block):
        sl = slice(j * block, (j + 1) * block)
        xr = dot_t(big_ref[:span, :], g_ref[sl, :])
        xi = dot_t(big_ref[span:, :], g_ref[sl, :])
        hr = filt_ref[:span, sl]
        hi = filt_ref[span:, sl]
        yf_ref[:span, sl] = (hr * xr + hi * xi).astype(BF16)
        yf_ref[span:, sl] = (hi * xr - hr * xi).astype(BF16)
        br = dot(big_ref[:span, :], yf_ref[:, sl])
        bi = dot(big_ref[span:, :], yf_ref[:, sl])
        b_ref[:, sl] = (br * twt_ref[0] - bi * twt_ref[1]).astype(BF16)
        b_ref[:, rows + j * block : rows + (j + 1) * block] = (
            br * twt_ref[1] + bi * twt_ref[0]
        ).astype(BF16)
    y_ref[...] = (dot_t(last_ref[...], b_ref[...]) * (1.0 / plan.total)).astype(BF16)


def transform(plan, u, filt, tables):
    rows, span = plan.rows, plan.span
    macs = 2 * (2 * rows * u.shape[0] * span + 4 * span * span * rows)
    return pl.pallas_call(
        functools.partial(transform_kernel, plan),
        out_shape=jax.ShapeDtypeStruct(u.shape, BF16),
        scratch_shapes=[
            pltpu.VMEM((rows, 2 * span), BF16),
            pltpu.VMEM((2 * span, rows), BF16),
            pltpu.VMEM((span, 2 * rows), BF16),
        ],
        cost_estimate=pl.CostEstimate(flops=2 * macs, bytes_accessed=6 * 1024 * 1024, transcendentals=0),
        compiler_params=pltpu.CompilerParams(vmem_limit_bytes=VMEM_LIMIT),
        name="transform",
    )(u, filt, *tables)


def final_kernel(y_ref, u_ref, gate_ref, skip_ref, out_ref):
    conv = y_ref[...].astype(F32).T
    u = u_ref[...].astype(F32)
    out_ref[...] = ((conv + u * skip_ref[...]) * gate_ref[...]).astype(BF16)


def finish(y, u, gate, skip):
    length, chans = u.shape
    return pl.pallas_call(
        final_kernel,
        out_shape=jax.ShapeDtypeStruct((length, chans), BF16),
        cost_estimate=pl.CostEstimate(
            flops=4 * length * chans, bytes_accessed=10 * length * chans, transcendentals=0
        ),
        compiler_params=pltpu.CompilerParams(vmem_limit_bytes=VMEM_LIMIT),
        name="finish",
    )(y, u, gate, skip)


def exchange(values, axes):
    return lax.all_to_all(values, axes, split_axis=0, concat_axis=0, tiled=True)


def on_device(plan, tables, eye, streams, short_weight, short_bias, spectrum, skip_gain):
    seq = plan.seq
    own = plan.own
    length = streams.shape[1]
    chans = streams.shape[2]
    parts = 4 * spectrum.shape[2]
    sent = transpose_spectrum(spectrum, eye, spectrum.shape[3] // 4)
    recv = exchange(sent.reshape(-1, own, parts), ("chan", "seq"))
    filt = arrange_filter(recv)

    route = [(i, i + 1) for i in range(seq - 1)]
    halo = lax.ppermute(streams[:, length - 2 :, :], "seq", route)
    u, ut, gate = short_conv(streams, halo, short_weight, short_bias, eye)
    mine = exchange(ut.reshape(seq, own, length), "seq").reshape(seq * own, length)
    y = transform(plan, mine, filt, tables)
    back = exchange(y.reshape(seq, own, length), "seq").reshape(chans, length)
    return finish(back, u, gate, skip_gain[None, :])


def solution(mesh):
    seq = mesh.shape["seq"]
    chans = mesh.shape["chan"]
    plan = Plan(seq, chans, 16384, 4096)
    eye = jnp.asarray(np.eye(256), BF16)
    tw = plan.twiddle()
    twt = np.tile(tw.transpose(0, 2, 1), (1, 1, 4))
    tables = (
        jnp.asarray(plan.first_table(), BF16),
        jnp.asarray(plan.big_table(), BF16),
        jnp.asarray(tw, F32),
        jnp.asarray(twt, F32),
        jnp.asarray(plan.last_table(), BF16),
    )
    placed = (
        P(None, "seq", "chan"),
        P(None, None, "chan"),
        P(None, "chan"),
        P(None, None, ("chan", "seq"), None),
        P("chan"),
    )
    return jax.shard_map(
        functools.partial(on_device, plan, tables, eye),
        mesh=mesh,
        in_specs=placed,
        out_specs=P("seq", "chan"),
        check_vma=False,
    )
```

```python
import functools

import jax
import jax.numpy as jnp
import numpy as np
from jax import lax
from jax.experimental import pallas as pl
from jax.experimental.pallas import tpu as pltpu
from jax.sharding import PartitionSpec as P

F32 = jnp.float32
BF16 = jnp.bfloat16
VMEM_LIMIT = 20 * 1024 * 1024
VMEM_WHOLE = 56 * 1024 * 1024


def dot_t(lhs, rhs):
    return lax.dot_general(lhs, rhs, (((1,), (1,)), ((), ())), preferred_element_type=F32)


def dot(lhs, rhs):
    return jnp.dot(lhs, rhs, preferred_element_type=F32)


class Plan:
    def __init__(self, seq, chans, tokens, channels, groups):
        self.seq = seq
        self.own = channels // (seq * chans)
        self.span = tokens // seq
        self.total = 2 * tokens
        self.groups = groups
        self.members = self.own // groups
        self.spare = 16
        self.base = self.members * seq
        self.rows = self.base + self.spare
        q = np.arange(seq)
        half = seq // 2
        self.lows = 2 * (q % half) + q // half

    def stage_table(self):
        out = np.zeros((self.groups, 2, self.rows, self.seq, self.own))
        s = np.arange(self.seq)
        for ch in range(self.own):
            g, c = divmod(ch, self.members)
            at = [c * self.seq + q for q in range(self.seq)] + [self.base + c]
            low = np.append(self.lows, self.seq)
            angle = 2.0 * np.pi * ((low[:, None] * s) % (2 * self.seq)) / (2 * self.seq)
            out[g, 0, at, :, ch] = np.cos(angle)
            out[g, 1, at, :, ch] = np.sin(angle)
        return out

    def first_table(self):
        return self.stage_table().reshape(-1, self.seq * self.own)

    def last_table(self):
        table = self.stage_table() / self.total
        table[:, 1] *= -1.0
        return table.reshape(-1, self.seq * self.own).T

    def big_table(self):
        d = np.arange(self.span)
        angle = 2.0 * np.pi * ((d[:, None] * d[None, :]) % self.span) / self.span
        return np.concatenate([np.cos(angle), np.sin(angle)])

    def twiddle(self):
        low = np.append(self.lows, [self.seq] * self.spare)
        a = np.arange(self.span)
        angle = 2.0 * np.pi * ((low[:, None] * a[None, :]) % self.total) / self.total
        return np.stack([np.cos(angle), np.sin(angle)])

    def fold_table(self):
        half = self.seq
        lanes = 4 * self.seq
        out = np.zeros((2 * self.seq + 8, 2 * lanes))

        def lane(part, low):
            return part * 2 * half + (low % 2) * half + low // 2

        for q, low in enumerate(self.lows):
            for part in range(2):
                out[part * self.seq + q, lane(part, low)] = 1.0
                if low:
                    out[part * self.seq + q, lanes + lane(part, 2 * self.seq - low)] = 1.0 - 2.0 * part
        for part in range(2):
            out[2 * self.seq + part, lane(part, self.seq)] = 1.0
        return out


def spectrum_kernel(spec_ref, out_ref, held_ref, turned_ref, in_sems, out_sems):
    steps, _, _, _, wide = held_ref.shape
    fetches = [
        pltpu.make_async_copy(
            spec_ref.at[:, :, :, pl.ds(j * wide, wide)], held_ref.at[j], in_sems.at[j]
        )
        for j in range(steps)
    ]
    stores = [
        pltpu.make_async_copy(
            turned_ref.at[j], out_ref.at[pl.ds(j * wide, wide), :], out_sems.at[j]
        )
        for j in range(steps)
    ]
    for fetch in fetches:
        fetch.start()
    for j in range(steps):
        fetches[j].wait()
        rows = [held_ref[j, r, i] for i in range(2) for r in range(2)]
        turned_ref[j] = jnp.concatenate(rows, axis=0).T
        stores[j].start()
    for store in stores:
        store.wait()


def transpose_spectrum(spectrum, steps):
    rows = 4 * spectrum.shape[2]
    chans = spectrum.shape[3]
    return pl.pallas_call(
        spectrum_kernel,
        in_specs=[pl.BlockSpec(memory_space=pl.ANY)],
        out_specs=pl.BlockSpec(memory_space=pl.ANY),
        out_shape=jax.ShapeDtypeStruct((chans, rows), BF16),
        scratch_shapes=[
            pltpu.VMEM((steps, 2, 2, spectrum.shape[2], chans // steps), BF16),
            pltpu.VMEM((steps, chans // steps, rows), BF16),
            pltpu.SemaphoreType.DMA((steps,)),
            pltpu.SemaphoreType.DMA((steps,)),
        ],
        cost_estimate=pl.CostEstimate(
            flops=rows * chans, bytes_accessed=4 * rows * chans, transcendentals=0
        ),
        compiler_params=pltpu.CompilerParams(vmem_limit_bytes=VMEM_WHOLE),
        name="transpose_spectrum",
    )(spectrum)


def short(stream, halo, weight, bias):
    row = lax.broadcasted_iota(jnp.int32, stream.shape, 0)
    now = stream.astype(F32)
    before = halo.astype(F32)
    one = jnp.where(row == 0, before[1:2, :], pltpu.roll(now, 1, 0))
    two = pltpu.roll(now, 2, 0)
    two = jnp.where(row == 0, before[0:1, :], jnp.where(row == 1, before[1:2, :], two))
    return weight[0:1] * now + weight[1:2] * one + weight[2:3] * two + bias


def conv_kernel(streams_ref, halo_ref, weight_ref, bias_ref, skip_ref, ut_ref, direct_ref, gate_ref):
    def stream(k):
        return short(streams_ref[k], halo_ref[k], weight_ref[:, k, :], bias_ref[k : k + 1, :])

    u = (stream(1) * stream(2)).astype(BF16)
    ut_ref[...] = u.T
    direct_ref[...] = u.astype(F32) * skip_ref[...]
    gate_ref[...] = stream(0)


def short_conv(streams, halo, weight, bias, skip):
    _, length, chans = streams.shape
    return pl.pallas_call(
        conv_kernel,
        out_shape=(
            jax.ShapeDtypeStruct((chans, length), BF16),
            jax.ShapeDtypeStruct((length, chans), F32),
            jax.ShapeDtypeStruct((length, chans), F32),
        ),
        cost_estimate=pl.CostEstimate(
            flops=20 * length * chans, bytes_accessed=16 * length * chans, transcendentals=0
        ),
        compiler_params=pltpu.CompilerParams(vmem_limit_bytes=VMEM_LIMIT),
        name="short_conv",
    )(streams, halo, weight, bias, skip)


def filter_kernel(plan, recv_ref, fold_ref, out_ref, wide_ref):
    depth = recv_ref.shape[0]
    seq, rows, base = plan.seq, plan.rows, plan.base
    wide_ref[...] = recv_ref[...].astype(F32)
    row = lax.broadcasted_iota(jnp.int32, (depth, depth), 0)
    column = lax.broadcasted_iota(jnp.int32, (depth, depth), 1)
    reverse = jnp.where(row + column == depth - 1, 1.0, 0.0).astype(BF16)
    for g in range(plan.groups):
        for part in range(2):
            first = (2 * g + part) * rows + base
            out_ref[first : first + plan.spare, :] = jnp.zeros((plan.spare, depth), BF16)
    for ch in range(plan.own):
        g, c = divmod(ch, plan.members)
        turned = wide_ref[:, ch, :].astype(BF16).T
        back = dot(turned, reverse).astype(BF16)
        folded = dot(fold_ref[...], jnp.concatenate([turned, back], axis=0)).astype(BF16)
        for part in range(2):
            first = (2 * g + part) * rows
            out_ref[first + c * seq : first + (c + 1) * seq, :] = folded[part * seq : (part + 1) * seq]
            at = 2 * seq + part
            out_ref[first + base + c : first + base + c + 1, :] = folded[at : at + 1]


def arrange_filter(plan, recv, fold):
    depth, own, lanes = recv.shape
    return pl.pallas_call(
        functools.partial(filter_kernel, plan),
        out_shape=jax.ShapeDtypeStruct((2 * plan.groups * plan.rows, depth), BF16),
        scratch_shapes=[pltpu.VMEM((depth, own, lanes), F32)],
        cost_estimate=pl.CostEstimate(
            flops=2 * depth * own * lanes * depth, bytes_accessed=6 * depth * own * lanes, transcendentals=0
        ),
        compiler_params=pltpu.CompilerParams(vmem_limit_bytes=VMEM_LIMIT),
        name="arrange_filter",
    )(recv, fold)


def transform_kernel(plan, *refs):
    count = 6
    sources, y_ref, held = refs[:count], refs[count], refs[count + 1 : 2 * count + 1]
    left_ref, b_ref, sems = refs[2 * count + 1 :]
    fetches = [pltpu.make_async_copy(s, h, sems.at[j]) for j, (s, h) in enumerate(zip(sources, held))]
    for fetch in fetches:
        fetch.start()
    u_ref, first_ref, tw_ref, big_ref, filt_ref, last_ref = held
    seq, rows, base, span = plan.seq, plan.rows, plan.base, plan.span
    fetches[0].wait()
    fetches[1].wait()
    u = u_ref[...]
    stages = [
        dot(first_ref[2 * g * rows : 2 * (g + 1) * rows, :], u) for g in range(plan.groups)
    ]
    fetches[2].wait()

    def turn(re, im):
        parts = []
        for at in list(range(0, base, seq)) + [base]:
            size = seq if at < base else plan.spare
            first = 0 if at < base else seq
            c = tw_ref[0, first : first + size, :]
            s = tw_ref[1, first : first + size, :]
            r, i = re[at : at + size], im[at : at + size]
            parts.append((r * c - i * s, r * s + i * c))
        return [jnp.concatenate(p, axis=0).astype(BF16) for p in zip(*parts)]

    def multiply(re, im):
        left_ref[:rows, :span] = re
        left_ref[:rows, span:] = -im
        left_ref[rows:, :span] = im
        left_ref[rows:, span:] = re
        out = dot(left_ref[...], big_ref[...])
        return out[:rows], out[rows:]

    turned = [turn(stage[:rows], stage[rows:]) for stage in stages]
    fetches[3].wait()
    fetches[4].wait()
    for g in range(plan.groups):
        lo, mid, hi = (2 * g) * rows, (2 * g + 1) * rows, (2 * g + 2) * rows
        xr, xi = multiply(*turned[g])
        hr = filt_ref[lo:mid, :].astype(F32)
        h_im = filt_ref[mid:hi, :].astype(F32)
        yr = (hr * xr + h_im * xi).astype(BF16)
        yi = (h_im * xr - hr * xi).astype(BF16)
        br, bi = turn(*multiply(yr, yi))
        b_ref[lo:mid, :] = br
        b_ref[mid:hi, :] = bi
    fetches[5].wait()
    y_ref[...] = dot(last_ref[...], b_ref[...]).astype(BF16)


def transform(plan, u, filt, tables):
    rows, span = plan.groups * plan.rows, plan.span
    macs = 2 * (2 * rows * u.shape[0] * span + 4 * span * span * rows)
    first, tw, big, last = tables
    sources = (u, first, tw, big, filt, last)
    return pl.pallas_call(
        functools.partial(transform_kernel, plan),
        in_specs=[pl.BlockSpec(memory_space=pl.ANY)] * len(sources),
        out_specs=pl.BlockSpec(memory_space=pltpu.VMEM),
        out_shape=jax.ShapeDtypeStruct(u.shape, BF16),
        scratch_shapes=[pltpu.VMEM(s.shape, s.dtype) for s in sources]
        + [
            pltpu.VMEM((2 * plan.rows, 2 * span), BF16),
            pltpu.VMEM((2 * rows, span), BF16),
            pltpu.SemaphoreType.DMA((len(sources),)),
        ],
        cost_estimate=pl.CostEstimate(flops=2 * macs, bytes_accessed=6 * 1024 * 1024, transcendentals=0),
        compiler_params=pltpu.CompilerParams(vmem_limit_bytes=VMEM_WHOLE),
        name="transform",
    )(*sources)


def final_kernel(y_ref, direct_ref, gate_ref, out_ref):
    conv = y_ref[...].T.astype(F32)
    out_ref[...] = ((conv + direct_ref[...]) * gate_ref[...]).astype(BF16)


def finish(y, direct, gate):
    return pl.pallas_call(
        final_kernel,
        out_shape=jax.ShapeDtypeStruct(direct.shape, BF16),
        cost_estimate=pl.CostEstimate(
            flops=2 * direct.size, bytes_accessed=12 * direct.size, transcendentals=0
        ),
        compiler_params=pltpu.CompilerParams(vmem_limit_bytes=VMEM_LIMIT),
        name="finish",
    )(y, direct, gate)


def exchange(values, axes):
    return lax.all_to_all(values, axes, split_axis=0, concat_axis=0, tiled=True)


def on_device(plan, tables, fold, streams, short_weight, short_bias, spectrum, skip_gain):
    seq = plan.seq
    own = plan.own
    length = streams.shape[1]
    chans = streams.shape[2]
    parts = 4 * spectrum.shape[2]
    sent = transpose_spectrum(spectrum, 8)
    recv = exchange(sent.reshape(-1, own, parts), ("chan", "seq"))
    filt = arrange_filter(plan, recv, fold)

    route = [(i, i + 1) for i in range(seq - 1)]
    halo = lax.ppermute(streams[:, length - 2 :, :], "seq", route)
    ut, direct, gate = short_conv(streams, halo, short_weight, short_bias, skip_gain[None, :])
    mine = exchange(ut.reshape(seq, own, length), "seq").reshape(seq * own, length)
    y = transform(plan, mine, filt, tables)
    back = exchange(y.reshape(seq, own, length), "seq").reshape(chans, length)
    return finish(back, direct, gate)


def solution(mesh):
    seq = mesh.shape["seq"]
    chans = mesh.shape["chan"]
    plan = Plan(seq, chans, 16384, 4096, 1)
    fold = jnp.asarray(plan.fold_table(), BF16)
    tables = (
        jnp.asarray(plan.first_table(), BF16),
        jnp.asarray(plan.twiddle(), F32),
        jnp.asarray(plan.big_table(), BF16),
        jnp.asarray(plan.last_table(), BF16),
    )
    placed = (
        P(None, "seq", "chan"),
        P(None, None, "chan"),
        P(None, "chan"),
        P(None, None, ("chan", "seq"), None),
        P("chan"),
    )
    return jax.shard_map(
        functools.partial(on_device, plan, tables, fold),
        mesh=mesh,
        in_specs=placed,
        out_specs=P("seq", "chan"),
        check_vma=False,
    )
```

```python
import functools

import jax
import jax.numpy as jnp
import numpy as np
from jax import lax
from jax.experimental import pallas as pl
from jax.experimental.pallas import tpu as pltpu
from jax.sharding import PartitionSpec as P

F32 = jnp.float32
BF16 = jnp.bfloat16
VMEM_LIMIT = 20 * 1024 * 1024
VMEM_WHOLE = 53 * 1024 * 1024


def dot_t(lhs, rhs):
    return lax.dot_general(lhs, rhs, (((1,), (1,)), ((), ())), preferred_element_type=F32)


def dot(lhs, rhs):
    return jnp.dot(lhs, rhs, preferred_element_type=F32)


class Plan:
    def __init__(self, seq, chans, tokens, channels, groups):
        self.seq = seq
        self.own = channels // (seq * chans)
        self.span = tokens // seq
        self.total = 2 * tokens
        self.groups = groups
        self.members = self.own // groups
        self.spare = 16
        self.base = self.members * seq
        self.rows = self.base + self.spare
        q = np.arange(seq)
        half = seq // 2
        self.lows = 2 * (q % half) + q // half

    def stage_table(self):
        out = np.zeros((self.groups, 2, self.rows, self.seq, self.own))
        s = np.arange(self.seq)
        for ch in range(self.own):
            g, c = divmod(ch, self.members)
            at = [c * self.seq + q for q in range(self.seq)] + [self.base + c]
            low = np.append(self.lows, self.seq)
            angle = 2.0 * np.pi * ((low[:, None] * s) % (2 * self.seq)) / (2 * self.seq)
            out[g, 0, at, :, ch] = np.cos(angle)
            out[g, 1, at, :, ch] = np.sin(angle)
        return out

    def first_table(self):
        return self.stage_table().reshape(-1, self.seq * self.own)

    def last_table(self):
        table = self.stage_table() / self.total
        table[:, 1] *= -1.0
        return table.reshape(-1, self.seq * self.own).T

    def big_table(self):
        d = np.arange(self.span)
        angle = 2.0 * np.pi * ((d[:, None] * d[None, :]) % self.span) / self.span
        return np.concatenate([np.cos(angle), np.sin(angle)])

    def twiddle(self):
        low = np.append(self.lows, [self.seq] * self.spare)
        a = np.arange(self.span)
        angle = 2.0 * np.pi * ((low[:, None] * a[None, :]) % self.total) / self.total
        return np.stack([np.cos(angle), np.sin(angle)])

    def fold_table(self):
        half = self.seq
        lanes = 4 * self.seq
        out = np.zeros((2 * self.seq + 8, 2 * lanes))

        def lane(part, low):
            return part * 2 * half + (low % 2) * half + low // 2

        for q, low in enumerate(self.lows):
            for part in range(2):
                out[part * self.seq + q, lane(part, low)] = 1.0
                if low:
                    out[part * self.seq + q, lanes + lane(part, 2 * self.seq - low)] = 1.0 - 2.0 * part
        for part in range(2):
            out[2 * self.seq + part, lane(part, self.seq)] = 1.0
        return out


def spectrum_kernel(spec_ref, out_ref, held_ref, turned_ref, in_sems, out_sems):
    steps, _, _, _, wide = held_ref.shape
    fetches = [
        pltpu.make_async_copy(
            spec_ref.at[:, :, :, pl.ds(j * wide, wide)], held_ref.at[j], in_sems.at[j]
        )
        for j in range(steps)
    ]
    stores = [
        pltpu.make_async_copy(
            turned_ref.at[j], out_ref.at[pl.ds(j * wide, wide), :], out_sems.at[j]
        )
        for j in range(steps)
    ]
    for fetch in fetches:
        fetch.start()
    for j in range(steps):
        fetches[j].wait()
        rows = [held_ref[j, r, i] for i in range(2) for r in range(2)]
        turned_ref[j] = jnp.concatenate(rows, axis=0).T
        stores[j].start()
    for store in stores:
        store.wait()


def transpose_spectrum(spectrum, steps):
    rows = 4 * spectrum.shape[2]
    chans = spectrum.shape[3]
    return pl.pallas_call(
        spectrum_kernel,
        in_specs=[pl.BlockSpec(memory_space=pl.ANY)],
        out_specs=pl.BlockSpec(memory_space=pl.ANY),
        out_shape=jax.ShapeDtypeStruct((chans, rows), BF16),
        scratch_shapes=[
            pltpu.VMEM((steps, 2, 2, spectrum.shape[2], chans // steps), BF16),
            pltpu.VMEM((steps, chans // steps, rows), BF16),
            pltpu.SemaphoreType.DMA((steps,)),
            pltpu.SemaphoreType.DMA((steps,)),
        ],
        cost_estimate=pl.CostEstimate(
            flops=rows * chans, bytes_accessed=4 * rows * chans, transcendentals=0
        ),
        compiler_params=pltpu.CompilerParams(vmem_limit_bytes=VMEM_WHOLE),
        name="transpose_spectrum",
    )(spectrum)


def short(stream, halo, weight, bias):
    row = lax.broadcasted_iota(jnp.int32, stream.shape, 0)
    now = stream.astype(F32)
    before = halo.astype(F32)
    one = jnp.where(row == 0, before[1:2, :], pltpu.roll(now, 1, 0))
    two = pltpu.roll(now, 2, 0)
    two = jnp.where(row == 0, before[0:1, :], jnp.where(row == 1, before[1:2, :], two))
    return weight[0:1] * now + weight[1:2] * one + weight[2:3] * two + bias


def conv_kernel(streams_ref, halo_ref, weight_ref, bias_ref, skip_ref, ut_ref, direct_ref, gate_ref):
    def stream(k):
        return short(streams_ref[k], halo_ref[k], weight_ref[:, k, :], bias_ref[k : k + 1, :])

    u = (stream(1) * stream(2)).astype(BF16)
    ut_ref[...] = u.T
    direct_ref[...] = u.astype(F32) * skip_ref[...]
    gate_ref[...] = stream(0)


def short_conv(streams, halo, weight, bias, skip):
    _, length, chans = streams.shape
    return pl.pallas_call(
        conv_kernel,
        out_shape=(
            jax.ShapeDtypeStruct((chans, length), BF16),
            jax.ShapeDtypeStruct((length, chans), F32),
            jax.ShapeDtypeStruct((length, chans), F32),
        ),
        cost_estimate=pl.CostEstimate(
            flops=20 * length * chans, bytes_accessed=16 * length * chans, transcendentals=0
        ),
        compiler_params=pltpu.CompilerParams(vmem_limit_bytes=VMEM_LIMIT),
        name="short_conv",
    )(streams, halo, weight, bias, skip)


def filter_kernel(plan, recv_ref, fold_ref, out_ref, wide_ref):
    depth = recv_ref.shape[0]
    seq, rows, base = plan.seq, plan.rows, plan.base
    wide_ref[...] = recv_ref[...].astype(F32)
    row = lax.broadcasted_iota(jnp.int32, (depth, depth), 0)
    column = lax.broadcasted_iota(jnp.int32, (depth, depth), 1)
    reverse = jnp.where(row + column == depth - 1, 1.0, 0.0).astype(BF16)
    for g in range(plan.groups):
        for part in range(2):
            first = (2 * g + part) * rows + base
            out_ref[first : first + plan.spare, :] = jnp.zeros((plan.spare, depth), BF16)
    for ch in range(plan.own):
        g, c = divmod(ch, plan.members)
        turned = wide_ref[:, ch, :].astype(BF16).T
        back = dot(turned, reverse).astype(BF16)
        folded = dot(fold_ref[...], jnp.concatenate([turned, back], axis=0)).astype(BF16)
        for part in range(2):
            first = (2 * g + part) * rows
            out_ref[first + c * seq : first + (c + 1) * seq, :] = folded[part * seq : (part + 1) * seq]
            at = 2 * seq + part
            out_ref[first + base + c : first + base + c + 1, :] = folded[at : at + 1]


def arrange_filter(plan, recv, fold):
    depth, own, lanes = recv.shape
    return pl.pallas_call(
        functools.partial(filter_kernel, plan),
        out_shape=jax.ShapeDtypeStruct((2 * plan.groups * plan.rows, depth), BF16),
        scratch_shapes=[pltpu.VMEM((depth, own, lanes), F32)],
        cost_estimate=pl.CostEstimate(
            flops=2 * depth * own * lanes * depth, bytes_accessed=6 * depth * own * lanes, transcendentals=0
        ),
        compiler_params=pltpu.CompilerParams(vmem_limit_bytes=VMEM_LIMIT),
        name="arrange_filter",
    )(recv, fold)


def transform_kernel(plan, *refs):
    count = 6
    sources, y_ref, held = refs[:count], refs[count], refs[count + 1 : 2 * count + 1]
    left_ref, b_ref, sems = refs[2 * count + 1 :]
    fetches = [
        pltpu.make_async_copy(
            s.at[:, : h.shape[1]] if len(h.shape) == 3 else s, h, sems.at[j]
        )
        for j, (s, h) in enumerate(zip(sources, held))
    ]
    for fetch in fetches:
        fetch.start()
    u_ref, first_ref, tw_ref, big_ref, filt_ref, last_ref = held
    seq, rows, base, span = plan.seq, plan.rows, plan.base, plan.span
    fetches[0].wait()
    fetches[1].wait()
    u = u_ref[...]
    stages = [
        dot(first_ref[2 * g * rows : 2 * (g + 1) * rows, :], u) for g in range(plan.groups)
    ]
    fetches[2].wait()

    def turn(re, im):
        parts = []
        for at in list(range(0, base, seq)) + [base]:
            size = seq if at < base else plan.spare
            first = 0 if at < base else seq
            c = tw_ref[0, first : first + size, :]
            s = tw_ref[1, first : first + size, :]
            r, i = re[at : at + size], im[at : at + size]
            parts.append((r * c - i * s, r * s + i * c))
        return [jnp.concatenate(p, axis=0).astype(BF16) for p in zip(*parts)]

    def multiply(re, im):
        left_ref[:rows, :span] = re
        left_ref[:rows, span:] = -im
        left_ref[rows:, :span] = im
        left_ref[rows:, span:] = re
        out = dot(left_ref[...], big_ref[...])
        return out[:rows], out[rows:]

    turned = [turn(stage[:rows], stage[rows:]) for stage in stages]
    fetches[3].wait()
    fetches[4].wait()
    for g in range(plan.groups):
        lo, mid, hi = (2 * g) * rows, (2 * g + 1) * rows, (2 * g + 2) * rows
        xr, xi = multiply(*turned[g])
        hr = filt_ref[lo:mid, :].astype(F32)
        h_im = filt_ref[mid:hi, :].astype(F32)
        yr = (hr * xr + h_im * xi).astype(BF16)
        yi = (h_im * xr - hr * xi).astype(BF16)
        br, bi = turn(*multiply(yr, yi))
        b_ref[lo:mid, :] = br
        b_ref[mid:hi, :] = bi
    fetches[5].wait()
    y_ref[...] = dot(last_ref[...], b_ref[...]).astype(BF16)


def transform(plan, u, filt, tables):
    rows, span = plan.groups * plan.rows, plan.span
    macs = 2 * (2 * rows * u.shape[0] * span + 4 * span * span * rows)
    first, tw, big, last = tables
    sources = (u, first, tw, big, filt, last)
    return pl.pallas_call(
        functools.partial(transform_kernel, plan),
        in_specs=[pl.BlockSpec(memory_space=pl.ANY)] * len(sources),
        out_specs=pl.BlockSpec(memory_space=pltpu.VMEM),
        out_shape=jax.ShapeDtypeStruct(u.shape, BF16),
        scratch_shapes=[pltpu.VMEM(s.shape, s.dtype) for s in (u, first)]
        + [pltpu.VMEM((2, plan.seq + plan.spare, span), F32)]
        + [pltpu.VMEM(s.shape, s.dtype) for s in (big, filt, last)]
        + [
            pltpu.VMEM((2 * plan.rows, 2 * span), BF16),
            pltpu.VMEM((2 * rows, span), BF16),
            pltpu.SemaphoreType.DMA((len(sources),)),
        ],
        cost_estimate=pl.CostEstimate(flops=2 * macs, bytes_accessed=6 * 1024 * 1024, transcendentals=0),
        compiler_params=pltpu.CompilerParams(vmem_limit_bytes=VMEM_WHOLE),
        name="transform",
    )(*sources)


def final_kernel(y_ref, direct_ref, gate_ref, out_ref):
    conv = y_ref[...].T.astype(F32)
    out_ref[...] = ((conv + direct_ref[...]) * gate_ref[...]).astype(BF16)


def finish(y, direct, gate):
    return pl.pallas_call(
        final_kernel,
        out_shape=jax.ShapeDtypeStruct(direct.shape, BF16),
        cost_estimate=pl.CostEstimate(
            flops=2 * direct.size, bytes_accessed=12 * direct.size, transcendentals=0
        ),
        compiler_params=pltpu.CompilerParams(vmem_limit_bytes=VMEM_LIMIT),
        name="finish",
    )(y, direct, gate)


def exchange(values, axes):
    return lax.all_to_all(values, axes, split_axis=0, concat_axis=0, tiled=True)


def on_device(plan, tables, fold, streams, short_weight, short_bias, spectrum, skip_gain):
    seq = plan.seq
    own = plan.own
    length = streams.shape[1]
    chans = streams.shape[2]
    parts = 4 * spectrum.shape[2]
    sent = transpose_spectrum(spectrum, 4)
    recv = exchange(sent.reshape(-1, own, parts), ("chan", "seq"))
    filt = arrange_filter(plan, recv, fold)

    route = [(i, i + 1) for i in range(seq - 1)]
    halo = lax.ppermute(streams[:, length - 2 :, :], "seq", route)
    ut, direct, gate = short_conv(streams, halo, short_weight, short_bias, skip_gain[None, :])
    mine = exchange(ut.reshape(seq, own, length), "seq").reshape(seq * own, length)
    y = transform(plan, mine, filt, tables)
    back = exchange(y.reshape(seq, own, length), "seq").reshape(chans, length)
    return finish(back, direct, gate)


def solution(mesh):
    seq = mesh.shape["seq"]
    chans = mesh.shape["chan"]
    plan = Plan(seq, chans, 16384, 4096, 1)
    fold = jnp.asarray(plan.fold_table(), BF16)
    tables = (
        jnp.asarray(plan.first_table(), BF16),
        jnp.asarray(np.pad(plan.twiddle(), ((0, 0), (0, 48), (0, 0))), F32),
        jnp.asarray(plan.big_table(), BF16),
        jnp.asarray(plan.last_table(), BF16),
    )
    placed = (
        P(None, "seq", "chan"),
        P(None, None, "chan"),
        P(None, "chan"),
        P(None, None, ("chan", "seq"), None),
        P("chan"),
    )
    return jax.shard_map(
        functools.partial(on_device, plan, tables, fold),
        mesh=mesh,
        in_specs=placed,
        out_specs=P("seq", "chan"),
        check_vma=False,
    )
```

```python
import functools

import jax
import jax.numpy as jnp
import numpy as np
from jax import lax
from jax.experimental import pallas as pl
from jax.experimental.pallas import tpu as pltpu
from jax.sharding import PartitionSpec as P

F32 = jnp.float32
BF16 = jnp.bfloat16
VMEM_LIMIT = 20 * 1024 * 1024
VMEM_WHOLE = 53 * 1024 * 1024


def dot_t(lhs, rhs):
    return lax.dot_general(lhs, rhs, (((1,), (1,)), ((), ())), preferred_element_type=F32)


def dot(lhs, rhs):
    return jnp.dot(lhs, rhs, preferred_element_type=F32)


class Plan:
    def __init__(self, seq, chans, tokens, channels, groups):
        self.seq = seq
        self.own = channels // (seq * chans)
        self.span = tokens // seq
        self.total = 2 * tokens
        self.groups = groups
        self.members = self.own // groups
        self.spare = 16
        self.base = self.members * seq
        self.rows = self.base + self.spare
        q = np.arange(seq)
        half = seq // 2
        self.lows = 2 * (q % half) + q // half

    def stage_table(self):
        out = np.zeros((self.groups, 2, self.rows, self.seq, self.own))
        s = np.arange(self.seq)
        for ch in range(self.own):
            g, c = divmod(ch, self.members)
            at = [c * self.seq + q for q in range(self.seq)] + [self.base + c]
            low = np.append(self.lows, self.seq)
            angle = 2.0 * np.pi * ((low[:, None] * s) % (2 * self.seq)) / (2 * self.seq)
            out[g, 0, at, :, ch] = np.cos(angle)
            out[g, 1, at, :, ch] = np.sin(angle)
        return out

    def first_table(self):
        return self.stage_table().reshape(-1, self.seq * self.own)

    def last_table(self):
        table = self.stage_table() / self.total
        table[:, 1] *= -1.0
        return table.reshape(-1, self.seq * self.own).T

    def big_table(self):
        half = self.span // 2
        d = np.arange(half)
        angle = 2.0 * np.pi * ((d[:, None] * d[None, :]) % half) / half
        return np.concatenate([np.cos(angle), np.sin(angle)])

    def twiddle(self):
        low = np.append(self.lows, [self.seq] * self.spare)
        a = np.arange(self.span)
        angle = 2.0 * np.pi * ((low[:, None] * a[None, :]) % self.total) / self.total
        step = np.tile(2.0 * np.pi * a / self.span, (8, 1))
        angle = np.concatenate([angle, step])
        return np.stack([np.cos(angle), np.sin(angle)])

    def fold_table(self):
        half = self.seq
        lanes = 4 * self.seq
        out = np.zeros((2, 2 * self.seq + self.spare, lanes))

        def lane(part, low):
            return part * 2 * half + (low % 2) * half + low // 2

        for q, low in enumerate(self.lows):
            for part in range(2):
                out[0, part * self.seq + q, lane(part, low)] = 1.0
                if low:
                    out[1, part * self.seq + q, lane(part, 2 * self.seq - low)] = 1.0 - 2.0 * part
        for part in range(2):
            out[0, 2 * self.seq + part, lane(part, self.seq)] = 1.0
        return out.reshape(-1, lanes)


def spectrum_kernel(spec_ref, out_ref, held_ref, turned_ref, in_sems, out_sems):
    steps, _, _, _, wide = held_ref.shape
    fetches = [
        pltpu.make_async_copy(
            spec_ref.at[:, :, :, pl.ds(j * wide, wide)], held_ref.at[j], in_sems.at[j]
        )
        for j in range(steps)
    ]
    stores = [
        pltpu.make_async_copy(
            turned_ref.at[j], out_ref.at[pl.ds(j * wide, wide), :], out_sems.at[j]
        )
        for j in range(steps)
    ]
    for fetch in fetches:
        fetch.start()
    for j in range(steps):
        fetches[j].wait()
        rows = [held_ref[j, r, i] for i in range(2) for r in range(2)]
        turned_ref[j] = jnp.concatenate(rows, axis=0).T
        stores[j].start()
    for store in stores:
        store.wait()


def transpose_spectrum(spectrum, steps):
    rows = 4 * spectrum.shape[2]
    chans = spectrum.shape[3]
    return pl.pallas_call(
        spectrum_kernel,
        in_specs=[pl.BlockSpec(memory_space=pl.ANY)],
        out_specs=pl.BlockSpec(memory_space=pl.ANY),
        out_shape=jax.ShapeDtypeStruct((chans, rows), BF16),
        scratch_shapes=[
            pltpu.VMEM((steps, 2, 2, spectrum.shape[2], chans // steps), BF16),
            pltpu.VMEM((steps, chans // steps, rows), BF16),
            pltpu.SemaphoreType.DMA((steps,)),
            pltpu.SemaphoreType.DMA((steps,)),
        ],
        cost_estimate=pl.CostEstimate(
            flops=rows * chans, bytes_accessed=4 * rows * chans, transcendentals=0
        ),
        compiler_params=pltpu.CompilerParams(vmem_limit_bytes=VMEM_WHOLE),
        name="transpose_spectrum",
    )(spectrum)


def short(stream, halo, weight, bias):
    row = lax.broadcasted_iota(jnp.int32, stream.shape, 0)
    now = stream.astype(F32)
    before = halo.astype(F32)
    one = jnp.where(row == 0, before[1:2, :], pltpu.roll(now, 1, 0))
    two = pltpu.roll(now, 2, 0)
    two = jnp.where(row == 0, before[0:1, :], jnp.where(row == 1, before[1:2, :], two))
    return weight[0:1] * now + weight[1:2] * one + weight[2:3] * two + bias


def conv_kernel(streams_ref, halo_ref, weight_ref, bias_ref, skip_ref, ut_ref, direct_ref, gate_ref):
    def stream(k):
        return short(streams_ref[k], halo_ref[k], weight_ref[:, k, :], bias_ref[k : k + 1, :])

    u = (stream(1) * stream(2)).astype(BF16)
    ut_ref[...] = u.T
    direct_ref[...] = u.astype(F32) * skip_ref[...]
    gate_ref[...] = stream(0)


def short_conv(streams, halo, weight, bias, skip):
    _, length, chans = streams.shape
    return pl.pallas_call(
        conv_kernel,
        out_shape=(
            jax.ShapeDtypeStruct((chans, length), BF16),
            jax.ShapeDtypeStruct((length, chans), F32),
            jax.ShapeDtypeStruct((length, chans), F32),
        ),
        cost_estimate=pl.CostEstimate(
            flops=20 * length * chans, bytes_accessed=16 * length * chans, transcendentals=0
        ),
        compiler_params=pltpu.CompilerParams(vmem_limit_bytes=VMEM_LIMIT),
        name="short_conv",
    )(streams, halo, weight, bias, skip)


def filter_kernel(plan, recv_ref, fold_ref, out_ref, wide_ref, both_ref):
    depth = recv_ref.shape[0]
    seq, rows, base = plan.seq, plan.rows, plan.base
    wide_ref[...] = recv_ref[...].astype(F32)
    row = lax.broadcasted_iota(jnp.int32, (depth, depth), 0)
    column = lax.broadcasted_iota(jnp.int32, (depth, depth), 1)
    source = jnp.where(column < depth // 2, 2 * column, 2 * column - depth + 1)
    forth = jnp.where(row == source, 1.0, 0.0)
    reverse = jnp.where(row + source == depth - 1, 1.0, 0.0)
    order = jnp.concatenate([forth, reverse], axis=0).astype(BF16)
    for g in range(plan.groups):
        for part in range(2):
            first = (2 * g + part) * rows + base
            out_ref[first : first + plan.spare, :] = jnp.zeros((plan.spare, depth), BF16)
    each = fold_ref.shape[0] // 2
    for ch in range(plan.own):
        picked = dot(fold_ref[...], wide_ref[:, ch, :].astype(BF16).T).astype(BF16)
        both_ref[ch * each : (ch + 1) * each, :depth] = picked[:each]
        both_ref[ch * each : (ch + 1) * each, depth:] = picked[each:]
    sums = dot(both_ref[...], order).astype(BF16)
    for ch in range(plan.own):
        g, c = divmod(ch, plan.members)
        folded = sums[ch * each : (ch + 1) * each]
        for part in range(2):
            first = (2 * g + part) * rows
            out_ref[first + c * seq : first + (c + 1) * seq, :] = folded[part * seq : (part + 1) * seq]
            at = 2 * seq + part
            out_ref[first + base + c : first + base + c + 1, :] = folded[at : at + 1]


def arrange_filter(plan, recv, fold):
    depth, own, lanes = recv.shape
    return pl.pallas_call(
        functools.partial(filter_kernel, plan),
        out_shape=jax.ShapeDtypeStruct((2 * plan.groups * plan.rows, depth), BF16),
        scratch_shapes=[
            pltpu.VMEM((depth, own, lanes), F32),
            pltpu.VMEM((own * fold.shape[0] // 2, 2 * depth), BF16),
        ],
        cost_estimate=pl.CostEstimate(
            flops=2 * depth * own * lanes * depth, bytes_accessed=6 * depth * own * lanes, transcendentals=0
        ),
        compiler_params=pltpu.CompilerParams(vmem_limit_bytes=VMEM_LIMIT),
        name="arrange_filter",
    )(recv, fold)


def transform_kernel(plan, *refs):
    count = 6
    sources, y_ref, held = refs[:count], refs[count], refs[count + 1 : 2 * count + 1]
    left_ref, b_ref, sems = refs[2 * count + 1 :]
    fetches = [
        pltpu.make_async_copy(
            s.at[:, : h.shape[1]] if len(h.shape) == 3 else s, h, sems.at[j]
        )
        for j, (s, h) in enumerate(zip(sources, held))
    ]
    for fetch in fetches:
        fetch.start()
    u_ref, first_ref, tw_ref, big_ref, filt_ref, last_ref = held
    seq, rows, base, span = plan.seq, plan.rows, plan.base, plan.span
    fetches[0].wait()
    fetches[1].wait()
    u = u_ref[...]
    stages = [
        dot(first_ref[2 * g * rows : 2 * (g + 1) * rows, :], u) for g in range(plan.groups)
    ]
    fetches[2].wait()

    half = span // 2

    def turn(re, im):
        parts = []
        for at in list(range(0, base, seq)) + [base]:
            size = seq if at < base else plan.spare
            first = 0 if at < base else seq
            c = tw_ref[0, first : first + size, :]
            s = tw_ref[1, first : first + size, :]
            r, i = re[at : at + size], im[at : at + size]
            parts.append((r * c - i * s, r * s + i * c))
        return [jnp.concatenate(p, axis=0) for p in zip(*parts)]

    def step(re, im):
        c = tw_ref[0, seq + plan.spare : seq + plan.spare + 1, :half]
        s = tw_ref[1, seq + plan.spare : seq + plan.spare + 1, :half]
        return re * c - im * s, re * s + im * c

    def multiply(pairs):
        for j, (re, im) in enumerate(pairs):
            at = 2 * j * rows
            re, im = re.astype(BF16), im.astype(BF16)
            left_ref[at : at + rows, :half] = re
            left_ref[at : at + rows, half:] = -im
            left_ref[at + rows : at + 2 * rows, :half] = im
            left_ref[at + rows : at + 2 * rows, half:] = re
        out = dot(left_ref[...], big_ref[...])
        return [
            (out[2 * j * rows : (2 * j + 1) * rows], out[(2 * j + 1) * rows : (2 * j + 2) * rows])
            for j in range(len(pairs))
        ]

    turned = [turn(stage[:rows], stage[rows:]) for stage in stages]
    fetches[3].wait()
    fetches[4].wait()
    for g in range(plan.groups):
        lo, mid, hi = (2 * g) * rows, (2 * g + 1) * rows, (2 * g + 2) * rows
        re, im = turned[g]
        even = (re[:, :half] + re[:, half:], im[:, :half] + im[:, half:])
        odd = step(re[:, :half] - re[:, half:], im[:, :half] - im[:, half:])
        weighted = []
        for j, (xr, xi) in enumerate(multiply([even, odd])):
            hr = filt_ref[lo:mid, j * half : (j + 1) * half].astype(F32)
            hi_part = filt_ref[mid:hi, j * half : (j + 1) * half].astype(F32)
            weighted.append((hr * xr + hi_part * xi, hi_part * xr - hr * xi))
        (er, ei), odd = multiply(weighted)
        sr, si = step(*odd)
        br, bi = turn(
            jnp.concatenate([er + sr, er - sr], axis=1), jnp.concatenate([ei + si, ei - si], axis=1)
        )
        b_ref[lo:mid, :] = br.astype(BF16)
        b_ref[mid:hi, :] = bi.astype(BF16)
    fetches[5].wait()
    y_ref[...] = dot(last_ref[...], b_ref[...]).astype(BF16)


def transform(plan, u, filt, tables):
    rows, span = plan.groups * plan.rows, plan.span
    macs = 2 * (2 * rows * u.shape[0] * span + 2 * span * span * rows)
    first, tw, big, last = tables
    sources = (u, first, tw, big, filt, last)
    return pl.pallas_call(
        functools.partial(transform_kernel, plan),
        in_specs=[pl.BlockSpec(memory_space=pl.ANY)] * len(sources),
        out_specs=pl.BlockSpec(memory_space=pltpu.VMEM),
        out_shape=jax.ShapeDtypeStruct(u.shape, BF16),
        scratch_shapes=[pltpu.VMEM(s.shape, s.dtype) for s in (u, first)]
        + [pltpu.VMEM((2, plan.seq + plan.spare + 8, span), F32)]
        + [pltpu.VMEM(s.shape, s.dtype) for s in (big, filt, last)]
        + [
            pltpu.VMEM((4 * plan.rows, span), BF16),
            pltpu.VMEM((2 * rows, span), BF16),
            pltpu.SemaphoreType.DMA((len(sources),)),
        ],
        cost_estimate=pl.CostEstimate(flops=2 * macs, bytes_accessed=6 * 1024 * 1024, transcendentals=0),
        compiler_params=pltpu.CompilerParams(vmem_limit_bytes=VMEM_WHOLE),
        name="transform",
    )(*sources)


def final_kernel(y_ref, direct_ref, gate_ref, out_ref):
    conv = y_ref[...].T.astype(F32)
    out_ref[...] = ((conv + direct_ref[...]) * gate_ref[...]).astype(BF16)


def finish(y, direct, gate):
    return pl.pallas_call(
        final_kernel,
        out_shape=jax.ShapeDtypeStruct(direct.shape, BF16),
        cost_estimate=pl.CostEstimate(
            flops=2 * direct.size, bytes_accessed=12 * direct.size, transcendentals=0
        ),
        compiler_params=pltpu.CompilerParams(vmem_limit_bytes=VMEM_LIMIT),
        name="finish",
    )(y, direct, gate)


def exchange(values, axes):
    return lax.all_to_all(values, axes, split_axis=0, concat_axis=0, tiled=True)


def on_device(plan, tables, fold, streams, short_weight, short_bias, spectrum, skip_gain):
    seq = plan.seq
    own = plan.own
    length = streams.shape[1]
    chans = streams.shape[2]
    parts = 4 * spectrum.shape[2]
    sent = transpose_spectrum(spectrum, 4)
    recv = exchange(sent.reshape(-1, own, parts), ("chan", "seq"))
    filt = arrange_filter(plan, recv, fold)

    route = [(i, i + 1) for i in range(seq - 1)]
    halo = lax.ppermute(streams[:, length - 2 :, :], "seq", route)
    ut, direct, gate = short_conv(streams, halo, short_weight, short_bias, skip_gain[None, :])
    mine = exchange(ut.reshape(seq, own, length), "seq").reshape(seq * own, length)
    y = transform(plan, mine, filt, tables)
    back = exchange(y.reshape(seq, own, length), "seq").reshape(chans, length)
    return finish(back, direct, gate)


def solution(mesh):
    seq = mesh.shape["seq"]
    chans = mesh.shape["chan"]
    plan = Plan(seq, chans, 16384, 4096, 1)
    fold = jnp.asarray(plan.fold_table(), BF16)
    tables = (
        jnp.asarray(plan.first_table(), BF16),
        jnp.asarray(np.pad(plan.twiddle(), ((0, 0), (0, 40), (0, 0))), F32),
        jnp.asarray(plan.big_table(), BF16),
        jnp.asarray(plan.last_table(), BF16),
    )
    placed = (
        P(None, "seq", "chan"),
        P(None, None, "chan"),
        P(None, "chan"),
        P(None, None, ("chan", "seq"), None),
        P("chan"),
    )
    return jax.shard_map(
        functools.partial(on_device, plan, tables, fold),
        mesh=mesh,
        in_specs=placed,
        out_specs=P("seq", "chan"),
        check_vma=False,
    )
```

```python
import functools

import jax
import jax.numpy as jnp
import numpy as np
from jax import lax
from jax.experimental import pallas as pl
from jax.experimental.pallas import tpu as pltpu
from jax.sharding import PartitionSpec as P

F32 = jnp.float32
BF16 = jnp.bfloat16
VMEM_LIMIT = 20 * 1024 * 1024
VMEM_WHOLE = 52 * 1024 * 1024


def dot_t(lhs, rhs):
    return lax.dot_general(lhs, rhs, (((1,), (1,)), ((), ())), preferred_element_type=F32)


def dot(lhs, rhs):
    return jnp.dot(lhs, rhs, preferred_element_type=F32)


class Plan:
    def __init__(self, seq, chans, tokens, channels, groups):
        self.seq = seq
        self.own = channels // (seq * chans)
        self.span = tokens // seq
        self.total = 2 * tokens
        self.groups = groups
        self.members = self.own // groups
        self.spare = 16
        self.base = self.members * seq
        self.rows = self.base + self.spare
        q = np.arange(seq)
        half = seq // 2
        self.lows = 2 * (q % half) + q // half

    def stage_table(self):
        out = np.zeros((self.groups, 2, self.rows, self.seq, self.own))
        s = np.arange(self.seq)
        for ch in range(self.own):
            g, c = divmod(ch, self.members)
            at = [c * self.seq + q for q in range(self.seq)] + [self.base + c]
            low = np.append(self.lows, self.seq)
            angle = 2.0 * np.pi * ((low[:, None] * s) % (2 * self.seq)) / (2 * self.seq)
            out[g, 0, at, :, ch] = np.cos(angle)
            out[g, 1, at, :, ch] = np.sin(angle)
        return out

    def first_table(self):
        return self.stage_table().reshape(-1, self.seq * self.own)

    def last_table(self):
        table = self.stage_table() / self.total
        table[:, 1] *= -1.0
        return table.reshape(-1, self.seq * self.own).T

    def big_table(self):
        half = self.span // 2
        d = np.arange(half)
        angle = 2.0 * np.pi * ((d[:, None] * d[None, :]) % half) / half
        return np.concatenate([np.cos(angle), np.sin(angle)])

    def twiddle(self):
        low = np.append(self.lows, [self.seq] * self.spare)
        a = np.arange(self.span)
        angle = 2.0 * np.pi * ((low[:, None] * a[None, :]) % self.total) / self.total
        step = np.tile(2.0 * np.pi * a / self.span, (8, 1))
        angle = np.concatenate([angle, step])
        return np.stack([np.cos(angle), np.sin(angle)])

    def fold_table(self):
        half = self.seq
        lanes = 4 * self.seq
        out = np.zeros((2, 2 * self.seq + self.spare, lanes))

        def lane(part, low):
            return part * 2 * half + (low % 2) * half + low // 2

        for q, low in enumerate(self.lows):
            for part in range(2):
                out[0, part * self.seq + q, lane(part, low)] = 1.0
                if low:
                    out[1, part * self.seq + q, lane(part, 2 * self.seq - low)] = 1.0 - 2.0 * part
        for part in range(2):
            out[0, 2 * self.seq + part, lane(part, self.seq)] = 1.0
        return out.reshape(-1, lanes)


def spectrum_kernel(spec_ref, out_ref, held_ref, turned_ref, in_sems, out_sems):
    steps, _, _, _, wide = held_ref.shape
    fetches = [
        pltpu.make_async_copy(
            spec_ref.at[:, :, :, pl.ds(j * wide, wide)], held_ref.at[j], in_sems.at[j]
        )
        for j in range(steps)
    ]
    stores = [
        pltpu.make_async_copy(
            turned_ref.at[j], out_ref.at[pl.ds(j * wide, wide), :], out_sems.at[j]
        )
        for j in range(steps)
    ]
    for fetch in fetches:
        fetch.start()
    for j in range(steps):
        fetches[j].wait()
        rows = [held_ref[j, r, i] for i in range(2) for r in range(2)]
        turned_ref[j] = jnp.concatenate(rows, axis=0).T
        stores[j].start()
    for store in stores:
        store.wait()


def transpose_spectrum(spectrum, steps):
    rows = 4 * spectrum.shape[2]
    chans = spectrum.shape[3]
    return pl.pallas_call(
        spectrum_kernel,
        in_specs=[pl.BlockSpec(memory_space=pl.ANY)],
        out_specs=pl.BlockSpec(memory_space=pl.ANY),
        out_shape=jax.ShapeDtypeStruct((chans, rows), BF16),
        scratch_shapes=[
            pltpu.VMEM((steps, 2, 2, spectrum.shape[2], chans // steps), BF16),
            pltpu.VMEM((steps, chans // steps, rows), BF16),
            pltpu.SemaphoreType.DMA((steps,)),
            pltpu.SemaphoreType.DMA((steps,)),
        ],
        cost_estimate=pl.CostEstimate(
            flops=rows * chans, bytes_accessed=4 * rows * chans, transcendentals=0
        ),
        compiler_params=pltpu.CompilerParams(vmem_limit_bytes=VMEM_WHOLE),
        name="transpose_spectrum",
    )(spectrum)


def short(stream, halo, weight, bias):
    row = lax.broadcasted_iota(jnp.int32, stream.shape, 0)
    now = stream.astype(F32)
    before = halo.astype(F32)
    one = jnp.where(row == 0, before[1:2, :], pltpu.roll(now, 1, 0))
    two = pltpu.roll(now, 2, 0)
    two = jnp.where(row == 0, before[0:1, :], jnp.where(row == 1, before[1:2, :], two))
    return weight[0:1] * now + weight[1:2] * one + weight[2:3] * two + bias


def conv_kernel(streams_ref, halo_ref, weight_ref, bias_ref, skip_ref, ut_ref, direct_ref, gate_ref):
    def stream(k):
        return short(streams_ref[k], halo_ref[k], weight_ref[:, k, :], bias_ref[k : k + 1, :])

    u = (stream(1) * stream(2)).astype(BF16)
    ut_ref[...] = u.T
    direct_ref[...] = u.astype(F32) * skip_ref[...]
    gate_ref[...] = stream(0)


def short_conv(streams, halo, weight, bias, skip):
    _, length, chans = streams.shape
    return pl.pallas_call(
        conv_kernel,
        out_shape=(
            jax.ShapeDtypeStruct((chans, length), BF16),
            jax.ShapeDtypeStruct((length, chans), F32),
            jax.ShapeDtypeStruct((length, chans), F32),
        ),
        cost_estimate=pl.CostEstimate(
            flops=20 * length * chans, bytes_accessed=16 * length * chans, transcendentals=0
        ),
        compiler_params=pltpu.CompilerParams(vmem_limit_bytes=VMEM_LIMIT),
        name="short_conv",
    )(streams, halo, weight, bias, skip)


def filter_kernel(plan, recv_ref, fold_ref, out_ref, wide_ref, both_ref):
    depth = recv_ref.shape[0]
    seq, rows, base = plan.seq, plan.rows, plan.base
    wide_ref[...] = recv_ref[...].astype(F32)
    row = lax.broadcasted_iota(jnp.int32, (depth, depth), 0)
    column = lax.broadcasted_iota(jnp.int32, (depth, depth), 1)
    source = jnp.where(column < depth // 2, 2 * column, 2 * column - depth + 1)
    forth = jnp.where(row == source, 1.0, 0.0)
    reverse = jnp.where(row + source == depth - 1, 1.0, 0.0)
    order = jnp.concatenate([forth, reverse], axis=0).astype(BF16)
    for g in range(plan.groups):
        for part in range(2):
            first = (2 * g + part) * rows + base
            out_ref[first : first + plan.spare, :] = jnp.zeros((plan.spare, depth), BF16)
    each = fold_ref.shape[0] // 2
    for ch in range(plan.own):
        picked = dot(fold_ref[...], wide_ref[:, ch, :].astype(BF16).T).astype(BF16)
        both_ref[ch * each : (ch + 1) * each, :depth] = picked[:each]
        both_ref[ch * each : (ch + 1) * each, depth:] = picked[each:]
    sums = dot(both_ref[...], order).astype(BF16)
    for ch in range(plan.own):
        g, c = divmod(ch, plan.members)
        folded = sums[ch * each : (ch + 1) * each]
        for part in range(2):
            first = (2 * g + part) * rows
            out_ref[first + c * seq : first + (c + 1) * seq, :] = folded[part * seq : (part + 1) * seq]
            at = 2 * seq + part
            out_ref[first + base + c : first + base + c + 1, :] = folded[at : at + 1]


def arrange_filter(plan, recv, fold):
    depth, own, lanes = recv.shape
    return pl.pallas_call(
        functools.partial(filter_kernel, plan),
        out_shape=jax.ShapeDtypeStruct((2 * plan.groups * plan.rows, depth), BF16),
        scratch_shapes=[
            pltpu.VMEM((depth, own, lanes), F32),
            pltpu.VMEM((own * fold.shape[0] // 2, 2 * depth), BF16),
        ],
        cost_estimate=pl.CostEstimate(
            flops=2 * depth * own * lanes * depth, bytes_accessed=6 * depth * own * lanes, transcendentals=0
        ),
        compiler_params=pltpu.CompilerParams(vmem_limit_bytes=VMEM_LIMIT),
        name="arrange_filter",
    )(recv, fold)


def transform_kernel(plan, *refs):
    u_ref, first_ref, tw_ref, filt_ref, *sources = refs[:6]
    y_ref, big_ref, last_ref, left_ref, b_ref, sems = refs[6:]
    fetches = [
        pltpu.make_async_copy(s.at[: h.shape[0]], h, sems.at[j])
        for j, (s, h) in enumerate(zip(sources, (big_ref, last_ref)))
    ]
    for fetch in fetches:
        fetch.start()
    seq, rows, base, span = plan.seq, plan.rows, plan.base, plan.span
    u = u_ref[...]
    stages = [
        dot(first_ref[2 * g * rows : 2 * (g + 1) * rows, :], u) for g in range(plan.groups)
    ]
    half = span // 2

    def turn(re, im):
        parts = []
        for at in list(range(0, base, seq)) + [base]:
            size = seq if at < base else plan.spare
            first = 0 if at < base else seq
            c = tw_ref[0, first : first + size, :]
            s = tw_ref[1, first : first + size, :]
            r, i = re[at : at + size], im[at : at + size]
            parts.append((r * c - i * s, r * s + i * c))
        return [jnp.concatenate(p, axis=0) for p in zip(*parts)]

    def step(re, im):
        c = tw_ref[0, seq + plan.spare : seq + plan.spare + 1, :half]
        s = tw_ref[1, seq + plan.spare : seq + plan.spare + 1, :half]
        return re * c - im * s, re * s + im * c

    def multiply(pairs):
        for j, (re, im) in enumerate(pairs):
            at = 2 * j * rows
            re, im = re.astype(BF16), im.astype(BF16)
            left_ref[at : at + rows, :half] = re
            left_ref[at : at + rows, half:] = -im
            left_ref[at + rows : at + 2 * rows, :half] = im
            left_ref[at + rows : at + 2 * rows, half:] = re
        out = dot(left_ref[...], big_ref[...])
        return [
            (out[2 * j * rows : (2 * j + 1) * rows], out[(2 * j + 1) * rows : (2 * j + 2) * rows])
            for j in range(len(pairs))
        ]

    turned = [turn(stage[:rows], stage[rows:]) for stage in stages]
    fetches[0].wait()
    for g in range(plan.groups):
        lo, mid, hi = (2 * g) * rows, (2 * g + 1) * rows, (2 * g + 2) * rows
        re, im = turned[g]
        even = (re[:, :half] + re[:, half:], im[:, :half] + im[:, half:])
        odd = step(re[:, :half] - re[:, half:], im[:, :half] - im[:, half:])
        weighted = []
        for j, (xr, xi) in enumerate(multiply([even, odd])):
            hr = filt_ref[lo:mid, j * half : (j + 1) * half].astype(F32)
            hi_part = filt_ref[mid:hi, j * half : (j + 1) * half].astype(F32)
            weighted.append((hr * xr + hi_part * xi, hi_part * xr - hr * xi))
        (er, ei), odd = multiply(weighted)
        sr, si = step(*odd)
        br, bi = turn(
            jnp.concatenate([er + sr, er - sr], axis=1), jnp.concatenate([ei + si, ei - si], axis=1)
        )
        b_ref[lo:mid, :] = br.astype(BF16)
        b_ref[mid:hi, :] = bi.astype(BF16)
    fetches[1].wait()
    y_ref[...] = dot(last_ref[...], b_ref[...]).astype(BF16)


def transform(plan, u, filt, tables):
    rows, span = plan.groups * plan.rows, plan.span
    macs = 2 * (2 * rows * u.shape[0] * span + 2 * span * span * rows)
    first, tw, big, last = tables
    whole = pl.BlockSpec(memory_space=pltpu.VMEM)
    return pl.pallas_call(
        functools.partial(transform_kernel, plan),
        in_specs=[whole] * 4 + [pl.BlockSpec(memory_space=pl.ANY)] * 2,
        out_specs=whole,
        out_shape=jax.ShapeDtypeStruct(u.shape, BF16),
        scratch_shapes=[
            pltpu.VMEM((span, span // 2), BF16),
            pltpu.VMEM((u.shape[0], last.shape[1]), BF16),
            pltpu.VMEM((4 * plan.rows, span), BF16),
            pltpu.VMEM((2 * rows, span), BF16),
            pltpu.SemaphoreType.DMA((2,)),
        ],
        cost_estimate=pl.CostEstimate(flops=2 * macs, bytes_accessed=6 * 1024 * 1024, transcendentals=0),
        compiler_params=pltpu.CompilerParams(vmem_limit_bytes=VMEM_WHOLE),
        name="transform",
    )(u, first, tw, filt, big, last)


def final_kernel(y_ref, direct_ref, gate_ref, out_ref):
    conv = y_ref[...].T.astype(F32)
    out_ref[...] = ((conv + direct_ref[...]) * gate_ref[...]).astype(BF16)


def finish(y, direct, gate):
    return pl.pallas_call(
        final_kernel,
        out_shape=jax.ShapeDtypeStruct(direct.shape, BF16),
        cost_estimate=pl.CostEstimate(
            flops=2 * direct.size, bytes_accessed=12 * direct.size, transcendentals=0
        ),
        compiler_params=pltpu.CompilerParams(vmem_limit_bytes=VMEM_LIMIT),
        name="finish",
    )(y, direct, gate)


def exchange(values, axes):
    return lax.all_to_all(values, axes, split_axis=0, concat_axis=0, tiled=True)


def on_device(plan, tables, fold, streams, short_weight, short_bias, spectrum, skip_gain):
    seq = plan.seq
    own = plan.own
    length = streams.shape[1]
    chans = streams.shape[2]
    parts = 4 * spectrum.shape[2]
    sent = transpose_spectrum(spectrum, 4)
    recv = exchange(sent.reshape(-1, own, parts), ("chan", "seq"))
    filt = arrange_filter(plan, recv, fold)

    route = [(i, i + 1) for i in range(seq - 1)]
    halo = lax.ppermute(streams[:, length - 2 :, :], "seq", route)
    ut, direct, gate = short_conv(streams, halo, short_weight, short_bias, skip_gain[None, :])
    mine = exchange(ut.reshape(seq, own, length), "seq").reshape(seq * own, length)
    y = transform(plan, mine, filt, tables)
    back = exchange(y.reshape(seq, own, length), "seq").reshape(chans, length)
    return finish(back, direct, gate)


def solution(mesh):
    seq = mesh.shape["seq"]
    chans = mesh.shape["chan"]
    plan = Plan(seq, chans, 16384, 4096, 1)
    fold = jnp.asarray(plan.fold_table(), BF16)
    tables = (
        jnp.asarray(plan.first_table(), BF16),
        jnp.asarray(plan.twiddle(), F32),
        jnp.asarray(np.pad(plan.big_table(), ((0, 2048), (0, 0))), BF16),
        jnp.asarray(np.pad(plan.last_table(), ((0, 1024), (0, 0))), BF16),
    )
    placed = (
        P(None, "seq", "chan"),
        P(None, None, "chan"),
        P(None, "chan"),
        P(None, None, ("chan", "seq"), None),
        P("chan"),
    )
    return jax.shard_map(
        functools.partial(on_device, plan, tables, fold),
        mesh=mesh,
        in_specs=placed,
        out_specs=P("seq", "chan"),
        check_vma=False,
    )
```

```python
import functools

import jax
import jax.numpy as jnp
import numpy as np
from jax import lax
from jax.experimental import pallas as pl
from jax.experimental.pallas import tpu as pltpu
from jax.sharding import PartitionSpec as P

F32 = jnp.float32
BF16 = jnp.bfloat16
VMEM_LIMIT = 20 * 1024 * 1024
VMEM_WHOLE = 52 * 1024 * 1024


def dot_t(lhs, rhs):
    return lax.dot_general(lhs, rhs, (((1,), (1,)), ((), ())), preferred_element_type=F32)


def dot(lhs, rhs):
    return jnp.dot(lhs, rhs, preferred_element_type=F32)


class Plan:
    def __init__(self, seq, chans, tokens, channels, groups):
        self.seq = seq
        self.own = channels // (seq * chans)
        self.span = tokens // seq
        self.total = 2 * tokens
        self.groups = groups
        self.members = self.own // groups
        self.spare = 16
        self.base = self.members * seq
        self.rows = self.base + self.spare
        q = np.arange(seq)
        half = seq // 2
        self.lows = 2 * (q % half) + q // half

    def stage_table(self):
        out = np.zeros((self.groups, 2, self.rows, self.seq, self.own))
        s = np.arange(self.seq)
        for ch in range(self.own):
            g, c = divmod(ch, self.members)
            at = [c * self.seq + q for q in range(self.seq)] + [self.base + c]
            low = np.append(self.lows, self.seq)
            angle = 2.0 * np.pi * ((low[:, None] * s) % (2 * self.seq)) / (2 * self.seq)
            out[g, 0, at, :, ch] = np.cos(angle)
            out[g, 1, at, :, ch] = np.sin(angle)
        return out

    def first_table(self):
        return self.stage_table().reshape(-1, self.seq * self.own)

    def last_table(self):
        table = self.stage_table() / self.total
        table[:, 1] *= -1.0
        return table.reshape(-1, self.seq * self.own).T

    def big_table(self):
        half = self.span // 2
        d = np.arange(half)
        angle = 2.0 * np.pi * ((d[:, None] * d[None, :]) % half) / half
        return np.concatenate([np.cos(angle), np.sin(angle)])

    def twiddle(self):
        low = np.append(self.lows, [self.seq] * self.spare)
        a = np.arange(self.span)
        angle = 2.0 * np.pi * ((low[:, None] * a[None, :]) % self.total) / self.total
        step = np.tile(2.0 * np.pi * a / self.span, (8, 1))
        angle = np.concatenate([angle, step])
        return np.stack([np.cos(angle), np.sin(angle)])

    def fold_table(self):
        half = self.seq
        lanes = 4 * self.seq
        out = np.zeros((2, 2 * self.seq + self.spare, lanes))

        def lane(part, low):
            return part * 2 * half + (low % 2) * half + low // 2

        for q, low in enumerate(self.lows):
            for part in range(2):
                out[0, part * self.seq + q, lane(part, low)] = 1.0
                if low:
                    out[1, part * self.seq + q, lane(part, 2 * self.seq - low)] = 1.0 - 2.0 * part
        for part in range(2):
            out[0, 2 * self.seq + part, lane(part, self.seq)] = 1.0
        return out.reshape(-1, lanes)


def spectrum_kernel(spec_ref, out_ref, held_ref, turned_ref, in_sems, out_sems):
    steps, _, _, _, wide = held_ref.shape
    fetches = [
        pltpu.make_async_copy(
            spec_ref.at[:, :, :, pl.ds(j * wide, wide)], held_ref.at[j], in_sems.at[j]
        )
        for j in range(steps)
    ]
    stores = [
        pltpu.make_async_copy(
            turned_ref.at[j], out_ref.at[pl.ds(j * wide, wide), :], out_sems.at[j]
        )
        for j in range(steps)
    ]
    for fetch in fetches:
        fetch.start()
    for j in range(steps):
        fetches[j].wait()
        rows = [held_ref[j, r, i] for i in range(2) for r in range(2)]
        turned_ref[j] = jnp.concatenate(rows, axis=0).T
        stores[j].start()
    for store in stores:
        store.wait()


def transpose_spectrum(spectrum, steps):
    rows = 4 * spectrum.shape[2]
    chans = spectrum.shape[3]
    return pl.pallas_call(
        spectrum_kernel,
        in_specs=[pl.BlockSpec(memory_space=pl.ANY)],
        out_specs=pl.BlockSpec(memory_space=pl.ANY),
        out_shape=jax.ShapeDtypeStruct((chans, rows), BF16),
        scratch_shapes=[
            pltpu.VMEM((steps, 2, 2, spectrum.shape[2], chans // steps), BF16),
            pltpu.VMEM((steps, chans // steps, rows), BF16),
            pltpu.SemaphoreType.DMA((steps,)),
            pltpu.SemaphoreType.DMA((steps,)),
        ],
        cost_estimate=pl.CostEstimate(
            flops=rows * chans, bytes_accessed=4 * rows * chans, transcendentals=0
        ),
        compiler_params=pltpu.CompilerParams(vmem_limit_bytes=VMEM_WHOLE),
        name="transpose_spectrum",
    )(spectrum)


def short(stream, halo, weight, bias):
    row = lax.broadcasted_iota(jnp.int32, stream.shape, 0)
    now = stream.astype(F32)
    before = halo.astype(F32)
    one = jnp.where(row == 0, before[1:2, :], pltpu.roll(now, 1, 0))
    two = pltpu.roll(now, 2, 0)
    two = jnp.where(row == 0, before[0:1, :], jnp.where(row == 1, before[1:2, :], two))
    return weight[0:1] * now + weight[1:2] * one + weight[2:3] * two + bias


def conv_kernel(streams_ref, halo_ref, weight_ref, bias_ref, skip_ref, ut_ref, direct_ref, gate_ref):
    def stream(k):
        return short(streams_ref[k], halo_ref[k], weight_ref[:, k, :], bias_ref[k : k + 1, :])

    u = (stream(1) * stream(2)).astype(BF16)
    ut_ref[...] = u.T
    direct_ref[...] = u.astype(F32) * skip_ref[...]
    gate_ref[...] = stream(0)


def short_conv(streams, halo, weight, bias, skip):
    _, length, chans = streams.shape
    return pl.pallas_call(
        conv_kernel,
        out_shape=(
            jax.ShapeDtypeStruct((chans, length), BF16),
            jax.ShapeDtypeStruct((length, chans), F32),
            jax.ShapeDtypeStruct((length, chans), F32),
        ),
        cost_estimate=pl.CostEstimate(
            flops=20 * length * chans, bytes_accessed=16 * length * chans, transcendentals=0
        ),
        compiler_params=pltpu.CompilerParams(vmem_limit_bytes=VMEM_LIMIT),
        name="short_conv",
    )(streams, halo, weight, bias, skip)


def filter_kernel(plan, recv_ref, fold_ref, out_ref, wide_ref, both_ref):
    depth = recv_ref.shape[0]
    seq, rows, base = plan.seq, plan.rows, plan.base
    wide_ref[...] = recv_ref[...].astype(F32)
    row = lax.broadcasted_iota(jnp.int32, (depth, depth), 0)
    column = lax.broadcasted_iota(jnp.int32, (depth, depth), 1)
    source = jnp.where(column < depth // 2, 2 * column, 2 * column - depth + 1)
    forth = jnp.where(row == source, 1.0, 0.0)
    reverse = jnp.where(row + source == depth - 1, 1.0, 0.0)
    order = jnp.concatenate([forth, reverse], axis=0).astype(BF16)
    for g in range(plan.groups):
        for part in range(2):
            first = (2 * g + part) * rows + base
            out_ref[first : first + plan.spare, :] = jnp.zeros((plan.spare, depth), BF16)
    each = fold_ref.shape[0] // 2
    for ch in range(plan.own):
        picked = dot(fold_ref[...], wide_ref[:, ch, :].astype(BF16).T).astype(BF16)
        both_ref[ch * each : (ch + 1) * each, :depth] = picked[:each]
        both_ref[ch * each : (ch + 1) * each, depth:] = picked[each:]
    sums = dot(both_ref[...], order).astype(BF16)
    for ch in range(plan.own):
        g, c = divmod(ch, plan.members)
        folded = sums[ch * each : (ch + 1) * each]
        for part in range(2):
            first = (2 * g + part) * rows
            out_ref[first + c * seq : first + (c + 1) * seq, :] = folded[part * seq : (part + 1) * seq]
            at = 2 * seq + part
            out_ref[first + base + c : first + base + c + 1, :] = folded[at : at + 1]


def arrange_filter(plan, recv, fold):
    depth, own, lanes = recv.shape
    return pl.pallas_call(
        functools.partial(filter_kernel, plan),
        out_shape=jax.ShapeDtypeStruct((2 * plan.groups * plan.rows, depth), BF16),
        scratch_shapes=[
            pltpu.VMEM((depth, own, lanes), F32),
            pltpu.VMEM((own * fold.shape[0] // 2, 2 * depth), BF16),
        ],
        cost_estimate=pl.CostEstimate(
            flops=2 * depth * own * lanes * depth, bytes_accessed=6 * depth * own * lanes, transcendentals=0
        ),
        compiler_params=pltpu.CompilerParams(vmem_limit_bytes=VMEM_LIMIT),
        name="arrange_filter",
    )(recv, fold)


def transform_kernel(plan, *refs):
    u_ref, first_ref, tw_ref, filt_ref, *sources = refs[:6]
    y_ref, big_ref, last_ref, left_ref, b_ref, sems = refs[6:]
    fetches = [
        pltpu.make_async_copy(s.at[: h.shape[0]], h, sems.at[j])
        for j, (s, h) in enumerate(zip(sources, (big_ref, last_ref)))
    ]
    for fetch in fetches:
        fetch.start()
    seq, rows, base, span = plan.seq, plan.rows, plan.base, plan.span
    u = u_ref[...]
    stages = [
        dot(first_ref[2 * g * rows : 2 * (g + 1) * rows, :], u) for g in range(plan.groups)
    ]
    half = span // 2

    def turn(re, im):
        parts = []
        for at in list(range(0, base, seq)) + [base]:
            size = seq if at < base else plan.spare
            first = 0 if at < base else seq
            c = tw_ref[0, first : first + size, :]
            s = tw_ref[1, first : first + size, :]
            r, i = re[at : at + size], im[at : at + size]
            parts.append((r * c - i * s, r * s + i * c))
        return [jnp.concatenate(p, axis=0) for p in zip(*parts)]

    def step(re, im):
        c = tw_ref[0, seq + plan.spare : seq + plan.spare + 1, :half]
        s = tw_ref[1, seq + plan.spare : seq + plan.spare + 1, :half]
        return re * c - im * s, re * s + im * c

    def multiply(pairs):
        for j, (re, im) in enumerate(pairs):
            at = 2 * j * rows
            re, im = re.astype(BF16), im.astype(BF16)
            left_ref[at : at + rows, :half] = re
            left_ref[at : at + rows, half:] = -im
            left_ref[at + rows : at + 2 * rows, :half] = im
            left_ref[at + rows : at + 2 * rows, half:] = re
        out = dot(left_ref[...], big_ref[...])
        return [
            (out[2 * j * rows : (2 * j + 1) * rows], out[(2 * j + 1) * rows : (2 * j + 2) * rows])
            for j in range(len(pairs))
        ]

    turned = [turn(stage[:rows], stage[rows:]) for stage in stages]
    for g in range(plan.groups):
        lo, mid, hi = (2 * g) * rows, (2 * g + 1) * rows, (2 * g + 2) * rows
        re, im = turned[g]
        even = (re[:, :half] + re[:, half:], im[:, :half] + im[:, half:])
        odd = step(re[:, :half] - re[:, half:], im[:, :half] - im[:, half:])
        if g == 0:
            fetches[0].wait()
        weighted = []
        for j, (xr, xi) in enumerate(multiply([even, odd])):
            hr = filt_ref[lo:mid, j * half : (j + 1) * half].astype(F32)
            hi_part = filt_ref[mid:hi, j * half : (j + 1) * half].astype(F32)
            weighted.append((hr * xr + hi_part * xi, hi_part * xr - hr * xi))
        (er, ei), odd = multiply(weighted)
        sr, si = step(*odd)
        br, bi = turn(
            jnp.concatenate([er + sr, er - sr], axis=1), jnp.concatenate([ei + si, ei - si], axis=1)
        )
        b_ref[lo:mid, :] = br.astype(BF16)
        b_ref[mid:hi, :] = bi.astype(BF16)
    fetches[1].wait()
    y_ref[...] = dot(last_ref[...], b_ref[...]).astype(BF16)


def transform(plan, u, filt, tables):
    rows, span = plan.groups * plan.rows, plan.span
    macs = 2 * (2 * rows * u.shape[0] * span + 2 * span * span * rows)
    first, tw, big, last = tables
    whole = pl.BlockSpec(memory_space=pltpu.VMEM)
    return pl.pallas_call(
        functools.partial(transform_kernel, plan),
        in_specs=[whole] * 4 + [pl.BlockSpec(memory_space=pl.ANY)] * 2,
        out_specs=whole,
        out_shape=jax.ShapeDtypeStruct(u.shape, BF16),
        scratch_shapes=[
            pltpu.VMEM((span, span // 2), BF16),
            pltpu.VMEM((u.shape[0], last.shape[1]), BF16),
            pltpu.VMEM((4 * plan.rows, span), BF16),
            pltpu.VMEM((2 * rows, span), BF16),
            pltpu.SemaphoreType.DMA((2,)),
        ],
        cost_estimate=pl.CostEstimate(flops=2 * macs, bytes_accessed=6 * 1024 * 1024, transcendentals=0),
        compiler_params=pltpu.CompilerParams(vmem_limit_bytes=VMEM_WHOLE),
        name="transform",
    )(u, first, tw, filt, big, last)


def final_kernel(y_ref, direct_ref, gate_ref, out_ref):
    conv = y_ref[...].T.astype(F32)
    out_ref[...] = ((conv + direct_ref[...]) * gate_ref[...]).astype(BF16)


def finish(y, direct, gate):
    return pl.pallas_call(
        final_kernel,
        out_shape=jax.ShapeDtypeStruct(direct.shape, BF16),
        cost_estimate=pl.CostEstimate(
            flops=2 * direct.size, bytes_accessed=12 * direct.size, transcendentals=0
        ),
        compiler_params=pltpu.CompilerParams(vmem_limit_bytes=VMEM_LIMIT),
        name="finish",
    )(y, direct, gate)


def exchange(values, axes):
    return lax.all_to_all(values, axes, split_axis=0, concat_axis=0, tiled=True)


def on_device(plan, tables, fold, streams, short_weight, short_bias, spectrum, skip_gain):
    seq = plan.seq
    own = plan.own
    length = streams.shape[1]
    chans = streams.shape[2]
    parts = 4 * spectrum.shape[2]
    sent = transpose_spectrum(spectrum, 4)
    recv = exchange(sent.reshape(-1, own, parts), ("chan", "seq"))
    filt = arrange_filter(plan, recv, fold)

    route = [(i, i + 1) for i in range(seq - 1)]
    halo = lax.ppermute(streams[:, length - 2 :, :], "seq", route)
    ut, direct, gate = short_conv(streams, halo, short_weight, short_bias, skip_gain[None, :])
    mine = exchange(ut.reshape(seq, own, length), "seq").reshape(seq * own, length)
    y = transform(plan, mine, filt, tables)
    back = exchange(y.reshape(seq, own, length), "seq").reshape(chans, length)
    return finish(back, direct, gate)


def solution(mesh):
    seq = mesh.shape["seq"]
    chans = mesh.shape["chan"]
    plan = Plan(seq, chans, 16384, 4096, 1)
    fold = jnp.asarray(plan.fold_table(), BF16)
    tables = (
        jnp.asarray(plan.first_table(), BF16),
        jnp.asarray(plan.twiddle(), F32),
        jnp.asarray(np.pad(plan.big_table(), ((0, 2048), (0, 0))), BF16),
        jnp.asarray(np.pad(plan.last_table(), ((0, 1024), (0, 0))), BF16),
    )
    placed = (
        P(None, "seq", "chan"),
        P(None, None, "chan"),
        P(None, "chan"),
        P(None, None, ("chan", "seq"), None),
        P("chan"),
    )
    return jax.shard_map(
        functools.partial(on_device, plan, tables, fold),
        mesh=mesh,
        in_specs=placed,
        out_specs=P("seq", "chan"),
        check_vma=False,
    )
```
